512 devices in a mesh: hst: 64 (over z, y_lo, core), dev: 8 (over y_hi, x).
Axes of the slice: x: 4, y: 8 (y_hi: 2, y_lo: 4; y = y_hi * 4 + y_lo), z: 8, core: 2. Of those that a mesh axis runs over, the one named last changes fastest.
Arguments:
- grad_out: bfloat16 [65536, 12288], P(('hst', 'dev')), may hold values from -24 to 24
- pre_act: bfloat16 [65536, 64], P(('hst', 'dev')), may hold values from -6 to 6
- down_rows: bfloat16 [12288, 64], P(('hst', 'dev')), may hold values from -0.0546875 to 0.0546875
- states: float32 [3, 163840, 128], P(None, ('hst', 'dev')), may hold values from -6 to 6
- partner_hosts: int32 [64, 2], replicated, may hold values from 0 to 63, as said below
- slice_start: int32 [64, 8], P('hst', 'dev'), may hold values from 0 to 64, as said below
Outputs:
- grad_bucket: float32 [12288, 64], P(('hst', 'dev'))
- grad_pre: bfloat16 [65536, 64], P(('hst', 'dev'))
- backup: float32 [3, 2, 131072, 128], P(None, None, ('hst', 'dev'))
The draws below stay inside these ranges and needn't reach their ends.
Inputs may be any that keep to these rules, and one draw needn't show every extreme that they name: Each column is a permutation of the hosts; partner_hosts[h, 0], partner_hosts[h, 1] and h are three different hosts. `slice_start`: every entry is a multiple of 8.
All inputs are finite; a program needn't handle non-finite values.
Results may differ from the reference program's by a relative error of at most 0.0027.
Values may be sent and summed in bfloat16 or wider, within the bound.
No kernel may reach another device: no remote copies, remote signals or barrier semaphores. Data moves between devices by JAX's collectives and lax.ppermute only.
A program may use at most 64 MiB of HBM per device.

```python
import jax
import jax.numpy as jnp
from jax import lax

D = 12288
BUCKET = 64
CKR = 256
SPARE = 64
LANES = 128
SHARD_ROWS = 320
TOKENS = 65536
N_HST = 64
N_DEV = 8


def draw_partner_hosts(key, part):
    key = jax.random.fold_in(key, 11)
    order = jax.random.permutation(key, N_HST).astype(jnp.int32)
    ranks = jnp.zeros((N_HST,), jnp.int32).at[order].set(jnp.arange(N_HST, dtype=jnp.int32))
    first = order[(ranks + 1) % N_HST]
    second = order[(ranks + 2) % N_HST]
    return jnp.stack([first, second], axis=1).astype(jnp.int32)


def draw_slice_start(key, part):
    key = jax.random.fold_in(key, 23)
    shuffled = jax.random.permutation(key, N_HST * N_DEV).astype(jnp.int32)
    values = shuffled % (SPARE // 8 + 1) * 8
    return values.reshape(N_HST, N_DEV).astype(jnp.int32)


def raised(entries, key, source, target, parts, factor):
    owner, partner = [(jnp.arange(entries.shape[dim]) // (entries.shape[dim] // parts)).reshape([-1 if axis == dim else 1 for axis in range(entries.ndim)]) for dim in (source, target)]
    chosen = jax.random.permutation(key, parts)[partner]
    strong = (owner == chosen) | (owner == (partner + parts // 2) % parts)
    return jnp.where(strong, factor * entries, entries)


def shard_levels(rng, dims, pieces, low, top_value):
    level, own = 1.0, jax.random.fold_in(rng, 6)
    for position, parts in pieces:
        steps = jnp.exp(jax.random.uniform(jax.random.fold_in(own, position), (parts,), jnp.float32, low / len(pieces), top_value / len(pieces)))
        level = level * jnp.repeat(steps, dims[position] // parts).reshape([-1 if axis == position else 1 for axis in range(len(dims))])
    return level


def centred(stream_key, shape, scale, limit, pieces=(), held_as=jnp.bfloat16):
    factor_of = shard_levels(stream_key, shape, pieces, -0.22, 0.18) if pieces else 1.0
    values = jax.random.normal(stream_key, shape, jnp.float32) * scale * factor_of
    return jnp.minimum(jnp.maximum(values, -limit), limit).astype(held_as)


def noise_with(key, dims, deviation, reach, pieces, heavy, kind=jnp.bfloat16):
    array = deviation * jax.random.normal(key, dims, jnp.float32)
    if pieces:
        array = array * shard_levels(key, dims, pieces, -0.22, 0.18)
    return jnp.clip(raised(array, jax.random.fold_in(key, 3), *heavy), -reach, reach).astype(kind)


def setup_inputs(seed: int = 0) -> dict:
    splits = jax.random.split(jax.random.key(seed), 7)
    grad_out = noise_with(splits[0], (TOKENS, D), 1.0, 24.0, ((0, 512),), (0, 1, 512, 6.0))
    pre_act = centred(splits[1], (TOKENS, BUCKET), 1.5, 6.0, ((0, 512),))
    down_rows = centred(splits[2], (D, BUCKET), D ** -0.5, 0.0546875, ((0, 512),))
    states = centred(splits[3], (3, (N_HST * N_DEV) * SHARD_ROWS, LANES), 1.0, 6.0, ((1, 512),), jnp.float32)
    partner_hosts = draw_partner_hosts(jax.random.fold_in(splits[6], 71), 0)
    slice_start = draw_slice_start(jax.random.fold_in(splits[6], 71), 0)
    return dict(grad_out=grad_out, pre_act=pre_act, down_rows=down_rows, states=states, partner_hosts=partner_hosts, slice_start=slice_start)


def gelu_value(inputs):
    cubic = inputs * inputs * inputs
    tangent = jnp.tanh(0.7978845608 * (inputs + 0.044715 * cubic))
    return 0.5 * inputs * (1.0 + tangent)


def gelu_slope(inputs):
    squared = inputs * inputs
    tangent = jnp.tanh(0.7978845608 * (inputs + 0.044715 * squared * inputs))
    return 0.5 * (1.0 + tangent) + 0.5 * inputs * (1.0 - tangent * tangent) * 0.7978845608 * (1.0 + 3.0 * 0.044715 * squared)


def reference(grad_out, pre_act, down_rows, states, partner_hosts, slice_start):
    device_count = N_HST * N_DEV
    pre_float = pre_act.astype(jnp.float32)
    activation = gelu_value(pre_float).astype(jnp.bfloat16)
    grad_bucket = jnp.dot(grad_out.T, activation, preferred_element_type=jnp.float32) / device_count
    backward = jnp.dot(grad_out, down_rows, preferred_element_type=jnp.float32)
    grad_pre = (backward * gelu_slope(pre_float)).astype(jnp.bfloat16)
    shards = states.reshape(3, device_count, SHARD_ROWS, LANES)
    starts = slice_start.reshape(device_count).astype(jnp.int32)

    def take_slice(shard, first_row):
        return lax.dynamic_slice_in_dim(shard, first_row, CKR, 1)

    slices = jax.vmap(take_slice, in_axes=(1, 0))(shards, starts)
    slices = slices.reshape(N_HST, N_DEV, 3, CKR, LANES)
    sources = jnp.arange(N_HST, dtype=jnp.int32)
    copies = []
    for replica in range(2):
        inverse = jnp.zeros((N_HST,), jnp.int32).at[partner_hosts[:, replica]].set(sources)
        held = slices[inverse]
        copies.append(jnp.transpose(held, (2, 0, 1, 3, 4)).reshape(3, device_count * CKR, LANES))
    backup = jnp.stack(copies, axis=1)
    return grad_bucket, grad_pre, backup
```

```python
import functools

import jax
import jax.numpy as jnp
from jax import lax
from jax.experimental import pallas as pl
from jax.experimental.pallas import tpu as pltpu
from jax.sharding import PartitionSpec as P

CKR = 256
F32 = jnp.float32
BF16 = jnp.bfloat16
VMEM = pl.BlockSpec(memory_space=pltpu.VMEM)
SMEM = pl.BlockSpec(memory_space=pltpu.SMEM)
LIMIT = 40 * 1024 * 1024


def gelu_value(inputs):
    cubic = inputs * inputs * inputs
    tangent = jnp.tanh(0.7978845608 * (inputs + 0.044715 * cubic))
    return 0.5 * inputs * (1.0 + tangent)


def gelu_slope(inputs):
    squared = inputs * inputs
    tangent = jnp.tanh(0.7978845608 * (inputs + 0.044715 * squared * inputs))
    return 0.5 * (1.0 + tangent) + 0.5 * inputs * (1.0 - tangent * tangent) * 0.7978845608 * (
        1.0 + 3.0 * 0.044715 * squared
    )


def lane_group(shape):
    return lax.broadcasted_iota(jnp.int32, shape, 1) // 32


def first_kernel(start_ref, states_ref, rows_ref, out_ref):
    start = pl.multiple_of(start_ref[0, 0], 8)
    rows = jnp.concatenate([rows_ref[...].astype(F32), jnp.zeros((24, 64), F32)], axis=1)
    group = lane_group((8, 128))
    packed = []
    for c in range(2):
        total = jnp.zeros((8, 128), F32)
        for g in range(3):
            moved = pltpu.roll(rows[8 * g : 8 * g + 8], (32 * (g - c)) % 128, 1)
            total = jnp.where(group == g, moved, total)
        packed.append(total)
    blank = jnp.zeros((4, 128), F32)
    for pair in range(32):
        tiles = []
        for i in range(3):
            tile = 3 * pair + i
            tiles.append(states_ref[tile // 32, pl.ds(start + tile % 32 * 8, 8), :])
        flat = jnp.concatenate(tiles, axis=0)
        for half in range(2):
            out_ref[2 * pair + half] = jnp.concatenate(
                [flat[12 * half : 12 * half + 12], packed[half], blank], axis=0
            ).astype(BF16)


def weight_kernel(got_ref, out_ref):
    group = lane_group((8, 128))

    def body(p, carry):
        out = [jnp.zeros((8, 128), F32)] * 3
        for q in range(4):
            piece = got_ref[q * 16 + p].astype(F32)[12:20]
            for g in range(3):
                moved = pltpu.roll(piece, (32 * (q - g)) % 128, 1)
                out[g] = jnp.where(group == q, moved, out[g])
        out_ref[p] = jnp.concatenate(out, axis=0).astype(BF16)
        return carry

    lax.fori_loop(0, 16, body, 0)


def second_kernel(inverse_ref, got_ref, sum_ref, other_ref, out_ref):
    group = lane_group((8, 128))

    def body(p, carry):
        total = sum_ref[p] + other_ref[p].astype(F32) * 4.0
        for q in range(4):
            packed = jnp.zeros((8, 128), F32)
            for g in range(3):
                moved = pltpu.roll(total[8 * g : 8 * g + 8], (32 * (g - q)) % 128, 1)
                packed = jnp.where(group == g, moved, packed)
            high = packed.astype(BF16).astype(F32)
            t = q * 16 + p
            first = got_ref[inverse_ref[0, t]].astype(F32)[:12]
            second = got_ref[inverse_ref[1, t]].astype(F32)[:12]
            out_ref[t] = jnp.concatenate([first, second, high, packed - high], axis=0).astype(BF16)
        return carry

    lax.fori_loop(0, 16, body, 0)


def last_kernel(scale, got_ref, backup_ref, grad_ref):
    totals = [jnp.zeros((8, 128), F32)] * 2
    for pair in range(32):
        blocks = [got_ref[2 * pair].astype(F32), got_ref[2 * pair + 1].astype(F32)]
        for c in range(2):
            totals[c] = totals[c] + (blocks[c][24:32] + blocks[c][32:40])
        for k in range(2):
            flat = jnp.concatenate([block[12 * k : 12 * k + 12] for block in blocks], axis=0)
            for i in range(3):
                tile = 3 * pair + i
                backup_ref[tile // 32, k, pl.ds(tile % 32 * 8, 8), :] = flat[8 * i : 8 * i + 8]
    group = lane_group((8, 128))
    for g in range(3):
        low = pltpu.roll(totals[0], (-32 * g) % 128, 1)
        high = pltpu.roll(totals[1], (32 - 32 * g) % 128, 1)
        grad_ref[pl.ds(8 * g, 8), :] = (jnp.where(group == 0, low, high) * scale)[:, :64]


def term_kernel(core_ref, pre_ref, g0, g1, g2, g3, own_ref, other_ref, right_ref):
    @pl.when(pl.program_id(0) == 0)
    def _():
        act = gelu_value(pre_ref[...].astype(F32))
        low = jnp.concatenate([act, jnp.zeros((128, 192), F32)], axis=1)
        lane = lax.broadcasted_iota(jnp.int32, (128, 256), 1)
        mine = core_ref[0]
        for q in range(4):
            a = pltpu.roll(low, 32 * q, 1)
            b = pltpu.roll(low, (32 * q - 32) % 256, 1)
            keep, send = jnp.where(mine == 0, a, b), jnp.where(mine == 0, b, a)
            send = pltpu.roll(send, 128, 1)
            both = jnp.where(
                lane // 32 == q, keep, jnp.where(lane // 32 == q + 4, send, 0.0)
            )
            right_ref[q] = both.astype(BF16)

    total = None
    for q, g in enumerate((g0, g1, g2, g3)):
        part = lax.dot_general(
            g[...], right_ref[q], (((0,), (0,)), ((), ())), preferred_element_type=F32
        )
        total = part if total is None else total + part
    for p in range(2):
        for yh in range(2):
            for x in range(4):
                at = ((p * 2 + yh) * 4 + x) * 24
                own_ref[x, yh, p] = total[at : at + 24, :128]
                other_ref[x, yh, p] = total[at : at + 24, 128:]


def back_kernel(place_ref, own_ref, other_ref, pre_ref, g0, g1, g2, g3, out_ref, weight_ref, acc_ref):
    step = pl.program_id(0)

    @pl.when(step == 0)
    def _():
        acc_ref[...] = jnp.zeros_like(acc_ref)

    mine = place_ref[1]
    for p in range(2):
        for yh in range(2):
            for x in range(4):
                at = ((p * 2 + yh) * 4 + x) * 24
                k = x ^ mine
                weight_ref[pl.ds(at, 24), :128] = own_ref[k, yh, p].astype(F32)
                weight_ref[pl.ds(at, 24), 128:] = other_ref[k, yh, p].astype(F32)
    weight = weight_ref[...].astype(BF16)
    for q, g in enumerate((g0, g1, g2, g3)):
        acc_ref[q] += jnp.dot(g[...], weight, preferred_element_type=F32)

    @pl.when(step == pl.num_programs(0) - 1)
    def _():
        lane = lax.broadcasted_iota(jnp.int32, (128, 256), 1)
        total = jnp.zeros((128, 256), F32)
        for q in range(4):
            total = jnp.where(lane // 32 % 4 == q, acc_ref[q], total)
        halves = []
        for c in range(2):
            half = total[:, 128 * c : 128 * c + 128]
            half = half + pltpu.roll(half, 64, 1)
            halves.append(half + pltpu.roll(half, 32, 1))
        is_low = lax.broadcasted_iota(jnp.int32, (128, 128), 1) // 32 % 2 == place_ref[0]
        both = jnp.where(is_low, halves[0], halves[1])[:, :64]
        out_ref[...] = (both * gelu_slope(pre_ref[...].astype(F32))).astype(BF16)


def call(kernel, out_shape, in_specs, **kwargs):
    return pl.pallas_call(
        kernel,
        out_shape=out_shape,
        in_specs=in_specs,
        out_specs=jax.tree.map(lambda _: VMEM, out_shape),
        compiler_params=pltpu.CompilerParams(vmem_limit_bytes=LIMIT),
        **kwargs,
    )


def grad_specs():
    return [pl.BlockSpec((128, 384), lambda s, c, q=q: (0, q * 8 + s)) for q in range(4)]


def shards(grad_out, pre_act, down_rows, states, partner_hosts, slice_start):
    axes = ("hst", "dev")
    core = lax.axis_index("hst") % 2
    x = lax.axis_index("dev") % 4
    yh = lax.axis_index("dev") // 4

    def flip(array, bits):
        return lax.ppermute(array, axes, [(i, i ^ bits) for i in range(512)])

    shape = jax.ShapeDtypeStruct
    send1 = call(first_kernel, shape((64, 24, 128), BF16), [SMEM, VMEM, VMEM])(
        slice_start, states, down_rows
    )
    got1 = lax.all_to_all(send1, "hst", 0, 0, tiled=True)

    blocks = pl.BlockSpec((4, 2, 2, 24, 128), lambda s, c: (0, 0, s, 0, 0))
    fixed = pl.BlockSpec((128, 64), lambda s, c: (0, 0))
    keep, send = pl.pallas_call(
        term_kernel,
        out_shape=[shape((4, 2, 16, 24, 128), F32)] * 2,
        grid_spec=pltpu.PrefetchScalarGridSpec(
            num_scalar_prefetch=1,
            grid=(8,),
            in_specs=[fixed] + grad_specs(),
            out_specs=[blocks, blocks],
            scratch_shapes=[pltpu.VMEM((4, 128, 256), BF16)],
        ),
        compiler_params=pltpu.CompilerParams(vmem_limit_bytes=LIMIT),
    )(core[None], pre_act, *[grad_out] * 4)
    arrived = flip(send, 8)

    def pick(k):
        return keep[x ^ k] + arrived[x ^ k]

    parts = [flip(pick(k).astype(jnp.float16), k) for k in (1, 2, 3)]
    summed = pick(0)
    for part in parts:
        summed = summed + part.astype(F32)
    mine = summed[yh]
    other = flip((summed[1 - yh] * 0.25).astype(jnp.float16), 4)

    sources = jnp.arange(64, dtype=jnp.int32)
    matches = partner_hosts[:, :, None] == sources[None, None, :]
    inverse = jnp.sum(jnp.where(matches, sources[:, None, None], 0), axis=0)
    send2 = call(second_kernel, shape((64, 40, 128), BF16), [SMEM, VMEM, VMEM, VMEM])(
        inverse, got1, mine, other.astype(F32)
    )
    got2 = lax.all_to_all(send2, "hst", 0, 0, tiled=True)
    backup, grad_bucket = call(
        functools.partial(last_kernel, 1.0 / 512),
        [shape((3, 2, CKR, 128), F32), shape((24, 64), F32)],
        [VMEM],
    )(got2)

    held = call(weight_kernel, shape((16, 24, 128), BF16), [VMEM])(got1)
    across = flip(held, 4)
    pair = jnp.where(yh == 0, jnp.stack([held, across]), jnp.stack([across, held]))
    own = jnp.stack([pair] + [flip(pair, k) for k in (1, 2, 3)])
    far = flip(own, 8)
    wide = pl.BlockSpec((4, 2, 2, 24, 128), lambda s, c: (0, 0, s, 0, 0))
    grad_pre = pl.pallas_call(
        back_kernel,
        out_shape=shape((128, 64), BF16),
        grid_spec=pltpu.PrefetchScalarGridSpec(
            num_scalar_prefetch=1,
            grid=(8,),
            in_specs=[wide, wide, fixed] + grad_specs(),
            out_specs=fixed,
            scratch_shapes=[pltpu.VMEM((384, 256), F32), pltpu.VMEM((4, 128, 256), F32)],
        ),
        compiler_params=pltpu.CompilerParams(vmem_limit_bytes=LIMIT),
    )(jnp.stack([core, x]), own, far, pre_act, *[grad_out] * 4)
    return (grad_bucket, grad_pre, backup)


def solution(mesh):
    return jax.shard_map(
        shards,
        mesh=mesh,
        in_specs=(
            P(("hst", "dev"), None),
            P(("hst", "dev"), None),
            P(("hst", "dev"), None),
            P(None, ("hst", "dev"), None),
            P(),
            P("hst", "dev"),
        ),
        out_specs=(
            P(("hst", "dev"), None),
            P(("hst", "dev"), None),
            P(None, None, ("hst", "dev"), None),
        ),
        check_vma=False,
    )
```

```python
import functools

import jax
import jax.numpy as jnp
from jax import lax
from jax.experimental import pallas as pl
from jax.experimental.pallas import tpu as pltpu
from jax.sharding import PartitionSpec as P

CKR = 256
F32 = jnp.float32
BF16 = jnp.bfloat16
VMEM = pl.BlockSpec(memory_space=pltpu.VMEM)
SMEM = pl.BlockSpec(memory_space=pltpu.SMEM)
LIMIT = 40 * 1024 * 1024


def gelu_value(inputs):
    cubic = inputs * inputs * inputs
    tangent = jnp.tanh(0.7978845608 * (inputs + 0.044715 * cubic))
    return 0.5 * inputs * (1.0 + tangent)


def gelu_slope(inputs):
    squared = inputs * inputs
    tangent = jnp.tanh(0.7978845608 * (inputs + 0.044715 * squared * inputs))
    return 0.5 * (1.0 + tangent) + 0.5 * inputs * (1.0 - tangent * tangent) * 0.7978845608 * (
        1.0 + 3.0 * 0.044715 * squared
    )


def lane_group(shape):
    return lax.broadcasted_iota(jnp.int32, shape, 1) // 32


def first_kernel(start_ref, states_ref, rows_ref, out_ref):
    start = pl.multiple_of(start_ref[0, 0], 8)
    rows = jnp.concatenate([rows_ref[...].astype(F32), jnp.zeros((24, 64), F32)], axis=1)
    group = lane_group((8, 128))
    packed = []
    for c in range(2):
        total = jnp.zeros((8, 128), F32)
        for g in range(3):
            moved = pltpu.roll(rows[8 * g : 8 * g + 8], (32 * (g - c)) % 128, 1)
            total = jnp.where(group == g, moved, total)
        packed.append(total)
    blank = jnp.zeros((4, 128), F32)
    for pair in range(32):
        tiles = []
        for i in range(3):
            tile = 3 * pair + i
            tiles.append(states_ref[tile // 32, pl.ds(start + tile % 32 * 8, 8), :])
        flat = jnp.concatenate(tiles, axis=0)
        for half in range(2):
            out_ref[2 * pair + half] = jnp.concatenate(
                [flat[12 * half : 12 * half + 12], packed[half], blank], axis=0
            ).astype(BF16)


def weight_kernel(got_ref, out_ref):
    group = lane_group((8, 128))
    for p in range(16):
        out = [jnp.zeros((8, 128), F32)] * 3
        for q in range(4):
            piece = got_ref[q * 16 + p].astype(F32)[12:20]
            for g in range(3):
                moved = pltpu.roll(piece, (32 * (q - g)) % 128, 1) if g != q else piece
                out[g] = jnp.where(group == q, moved, out[g])
        out_ref[p] = jnp.concatenate(out, axis=0).astype(BF16)


def second_kernel(inverse_ref, got_ref, sum_ref, other_ref, out_ref):
    group = lane_group((8, 128))
    for p in range(16):
        total = sum_ref[p] + other_ref[p] * 4.0
        for q in range(4):
            packed = jnp.zeros((8, 128), F32)
            for g in range(3):
                moved = total[8 * g : 8 * g + 8]
                if g != q:
                    moved = pltpu.roll(moved, (32 * (g - q)) % 128, 1)
                packed = jnp.where(group == g, moved, packed)
            t = q * 16 + p
            rows = [got_ref[inverse_ref[k, t]].astype(F32)[:12] for k in range(2)]
            out_ref[t] = jnp.concatenate(rows + [packed], axis=0).astype(BF16)


def last_kernel(scale, got_ref, backup_ref, grad_ref):
    totals = [jnp.zeros((8, 128), F32)] * 2
    for pair in range(32):
        blocks = [got_ref[2 * pair].astype(F32), got_ref[2 * pair + 1].astype(F32)]
        for c in range(2):
            totals[c] = totals[c] + blocks[c][24:]
        for k in range(2):
            flat = jnp.concatenate([block[12 * k : 12 * k + 12] for block in blocks], axis=0)
            for i in range(3):
                tile = 3 * pair + i
                backup_ref[tile // 32, k, pl.ds(tile % 32 * 8, 8), :] = flat[8 * i : 8 * i + 8]
    group = lane_group((8, 128))
    for g in range(3):
        low = pltpu.roll(totals[0], (-32 * g) % 128, 1)
        high = pltpu.roll(totals[1], (32 - 32 * g) % 128, 1)
        grad_ref[pl.ds(8 * g, 8), :] = (jnp.where(group == 0, low, high) * scale)[:, :64]


def term_kernel(core_ref, pre_ref, g0, g1, g2, g3, own_ref, other_ref, right_ref):
    @pl.when(pl.program_id(0) == 0)
    def _():
        act = gelu_value(pre_ref[...].astype(F32)).T
        low = jnp.concatenate([act, jnp.zeros((128, 192), F32)], axis=1)
        lane = lax.broadcasted_iota(jnp.int32, (128, 256), 1)
        mine = core_ref[0]
        for q in range(4):
            a = pltpu.roll(low, 32 * q, 1)
            b = pltpu.roll(low, (32 * q - 32) % 256, 1)
            keep, send = jnp.where(mine == 0, a, b), jnp.where(mine == 0, b, a)
            send = pltpu.roll(send, 128, 1)
            both = jnp.where(
                lane // 32 == q, keep, jnp.where(lane // 32 == q + 4, send, 0.0)
            )
            right_ref[q] = both.astype(BF16)

    total = None
    for q, g in enumerate((g0, g1, g2, g3)):
        part = lax.dot_general(
            g[...], right_ref[q], (((0,), (0,)), ((), ())), preferred_element_type=F32
        )
        total = part if total is None else total + part
    for p in range(2):
        for yh in range(2):
            for x in range(4):
                at = ((p * 2 + yh) * 4 + x) * 24
                own_ref[x, yh, p] = total[at : at + 24, :128]
                other_ref[x, yh, p] = total[at : at + 24, 128:]


def back_kernel(place_ref, own_ref, other_ref, pre_ref, g0, g1, g2, g3, out_ref, weight_ref, acc_ref):
    step = pl.program_id(0)

    @pl.when(step == 0)
    def _():
        acc_ref[...] = jnp.zeros_like(acc_ref)

    for p in range(2):
        for yh in range(2):
            j = yh ^ place_ref[1]
            for x in range(4):
                at = ((p * 2 + yh) * 4 + x) * 24
                weight_ref[pl.ds(at, 24), :128] = own_ref[x, j, p].astype(F32)
                weight_ref[pl.ds(at, 24), 128:] = other_ref[x, j, p].astype(F32)
    weight = weight_ref[...].astype(BF16)
    for q, g in enumerate((g0, g1, g2, g3)):
        acc_ref[q] += jnp.dot(g[...], weight, preferred_element_type=F32)

    @pl.when(step == pl.num_programs(0) - 1)
    def _():
        lane = lax.broadcasted_iota(jnp.int32, (128, 256), 1)
        total = jnp.zeros((128, 256), F32)
        for q in range(4):
            total = jnp.where(lane // 32 % 4 == q, acc_ref[q], total)
        halves = []
        for c in range(2):
            half = total[:, 128 * c : 128 * c + 128]
            half = half + pltpu.roll(half, 64, 1)
            halves.append(half + pltpu.roll(half, 32, 1))
        is_low = lax.broadcasted_iota(jnp.int32, (128, 128), 1) // 32 % 2 == place_ref[0]
        both = jnp.where(is_low, halves[0], halves[1]).T[:64]
        out_ref[...] = (both * gelu_slope(pre_ref[...].astype(F32))).astype(BF16)


def call(kernel, out_shape, in_specs, **kwargs):
    return pl.pallas_call(
        kernel,
        out_shape=out_shape,
        in_specs=in_specs,
        out_specs=jax.tree.map(lambda _: VMEM, out_shape),
        compiler_params=pltpu.CompilerParams(vmem_limit_bytes=LIMIT),
        **kwargs,
    )


def grad_specs():
    return [pl.BlockSpec((128, 384), lambda s, c, q=q: (0, q * 8 + s)) for q in range(4)]


def shards(grad_out, pre_act, down_rows, states, partner_hosts, slice_start):
    axes = ("hst", "dev")
    core = lax.axis_index("hst") % 2
    x = lax.axis_index("dev") % 4
    yh = lax.axis_index("dev") // 4

    def flip(array, bits):
        return lax.ppermute(array, axes, [(i, i ^ bits) for i in range(512)])

    shape = jax.ShapeDtypeStruct
    send1 = call(first_kernel, shape((64, 24, 128), BF16), [SMEM, VMEM, VMEM])(
        slice_start, states, down_rows
    )
    got1 = lax.all_to_all(send1, "hst", 0, 0, tiled=True)

    blocks = pl.BlockSpec((4, 2, 2, 24, 128), lambda s, c: (0, 0, s, 0, 0))
    fixed = pl.BlockSpec((64, 128), lambda s, c: (0, 0))
    keep, send = pl.pallas_call(
        term_kernel,
        out_shape=[shape((4, 2, 16, 24, 128), F32)] * 2,
        grid_spec=pltpu.PrefetchScalarGridSpec(
            num_scalar_prefetch=1,
            grid=(8,),
            in_specs=[fixed] + grad_specs(),
            out_specs=[blocks, blocks],
            scratch_shapes=[pltpu.VMEM((4, 128, 256), BF16)],
        ),
        compiler_params=pltpu.CompilerParams(vmem_limit_bytes=LIMIT),
    )(core[None], pre_act.T, *[grad_out] * 4)
    arrived = flip(send, 8)

    def pick(k):
        return keep[x ^ k] + arrived[x ^ k]

    leaving = [pick(k).astype(jnp.float16) for k in (1, 3, 2)]
    parts = [flip(part, k) for part, k in zip(leaving, (1, 3, 2))]
    got1, _ = lax.optimization_barrier((got1, parts[0]))
    summed = pick(0)
    for part in parts:
        summed = summed + part.astype(F32)
    mine = summed[yh]
    other = flip((summed[1 - yh] * 0.25).astype(jnp.float16), 4)

    sources = jnp.arange(64, dtype=jnp.int32)
    matches = partner_hosts[:, :, None] == sources[None, None, :]
    inverse = jnp.sum(jnp.where(matches, sources[:, None, None], 0), axis=0)
    held = call(weight_kernel, shape((16, 24, 128), BF16), [VMEM])(got1)
    across = flip(held, 4)
    inverse, _ = lax.optimization_barrier((inverse, across))
    send2 = call(second_kernel, shape((64, 32, 128), BF16), [SMEM, VMEM, VMEM, VMEM])(
        inverse, got1, mine, other.astype(F32)
    )
    got2 = lax.all_to_all(send2, "hst", 0, 0, tiled=True)
    backup, grad_bucket = call(
        functools.partial(last_kernel, 1.0 / 512),
        [shape((3, 2, CKR, 128), F32), shape((24, 64), F32)],
        [VMEM],
    )(got2)

    held, across, _ = lax.optimization_barrier((held, across, send2))
    pair = jnp.concatenate([held, across]).reshape(768, 128)
    lines = [[0, 1, 2, 3], [4, 5, 6, 7]]
    own = lax.all_gather(pair, "dev", axis=0, tiled=True, axis_index_groups=lines)
    own = own.reshape(4, 2, 16, 24, 128)
    far = flip(own, 8)
    wide = pl.BlockSpec((4, 2, 2, 24, 128), lambda s, c: (0, 0, s, 0, 0))
    grad_pre = pl.pallas_call(
        back_kernel,
        out_shape=shape((64, 128), BF16),
        grid_spec=pltpu.PrefetchScalarGridSpec(
            num_scalar_prefetch=1,
            grid=(8,),
            in_specs=[wide, wide, fixed] + grad_specs(),
            out_specs=fixed,
            scratch_shapes=[pltpu.VMEM((384, 256), F32), pltpu.VMEM((4, 128, 256), F32)],
        ),
        compiler_params=pltpu.CompilerParams(vmem_limit_bytes=LIMIT),
    )(jnp.stack([core, yh]), own, far, pre_act.T, *[grad_out] * 4)
    return (grad_bucket, grad_pre.T, backup)


def solution(mesh):
    return jax.shard_map(
        shards,
        mesh=mesh,
        in_specs=(
            P(("hst", "dev"), None),
            P(("hst", "dev"), None),
            P(("hst", "dev"), None),
            P(None, ("hst", "dev"), None),
            P(),
            P("hst", "dev"),
        ),
        out_specs=(
            P(("hst", "dev"), None),
            P(("hst", "dev"), None),
            P(None, None, ("hst", "dev"), None),
        ),
        check_vma=False,
    )
```

```python
import functools

import jax
import jax.numpy as jnp
from jax import lax
from jax.experimental import pallas as pl
from jax.experimental.pallas import tpu as pltpu
from jax.sharding import PartitionSpec as P

CKR = 256
F32 = jnp.float32
BF16 = jnp.bfloat16
VMEM = pl.BlockSpec(memory_space=pltpu.VMEM)
SMEM = pl.BlockSpec(memory_space=pltpu.SMEM)
LIMIT = 40 * 1024 * 1024


def gelu_value(inputs):
    cubic = inputs * inputs * inputs
    tangent = jnp.tanh(0.7978845608 * (inputs + 0.044715 * cubic))
    return 0.5 * inputs * (1.0 + tangent)


def gelu_slope(inputs):
    squared = inputs * inputs
    tangent = jnp.tanh(0.7978845608 * (inputs + 0.044715 * squared * inputs))
    return 0.5 * (1.0 + tangent) + 0.5 * inputs * (1.0 - tangent * tangent) * 0.7978845608 * (
        1.0 + 3.0 * 0.044715 * squared
    )


def lane_group(shape):
    return lax.broadcasted_iota(jnp.int32, shape, 1) // 32


def first_kernel(start_ref, states_ref, rows_ref, out_ref):
    start = pl.multiple_of(start_ref[0, 0], 8)
    rows = jnp.concatenate([rows_ref[...].astype(F32), jnp.zeros((24, 64), F32)], axis=1)
    group = lane_group((8, 128))
    packed = []
    for c in range(2):
        total = jnp.zeros((8, 128), F32)
        for g in range(3):
            moved = pltpu.roll(rows[8 * g : 8 * g + 8], (32 * (g - c)) % 128, 1)
            total = jnp.where(group == g, moved, total)
        packed.append(total)
    blank = jnp.zeros((4, 128), F32)
    for pair in range(32):
        tiles = []
        for i in range(3):
            tile = 3 * pair + i
            tiles.append(states_ref[tile // 32, pl.ds(start + tile % 32 * 8, 8), :])
        flat = jnp.concatenate(tiles, axis=0)
        for half in range(2):
            out_ref[2 * pair + half] = jnp.concatenate(
                [flat[12 * half : 12 * half + 12], packed[half], blank], axis=0
            ).astype(BF16)


def weight_kernel(got_ref, out_ref):
    group = lane_group((8, 128))
    for p in range(16):
        out = [jnp.zeros((8, 128), F32)] * 3
        for q in range(4):
            piece = got_ref[q * 16 + p].astype(F32)[12:20]
            for g in range(3):
                moved = pltpu.roll(piece, (32 * (q - g)) % 128, 1) if g != q else piece
                out[g] = jnp.where(group == q, moved, out[g])
        out_ref[p] = jnp.concatenate(out, axis=0).astype(BF16)


def second_kernel(inverse_ref, got_ref, sum_ref, other_ref, out_ref):
    group = lane_group((8, 128))
    for p in range(16):
        total = sum_ref[p] + other_ref[p] * 4.0
        for q in range(4):
            packed = jnp.zeros((8, 128), F32)
            for g in range(3):
                moved = total[8 * g : 8 * g + 8]
                if g != q:
                    moved = pltpu.roll(moved, (32 * (g - q)) % 128, 1)
                packed = jnp.where(group == g, moved, packed)
            t = q * 16 + p
            rows = [got_ref[inverse_ref[k, t]].astype(F32)[:12] for k in range(2)]
            out_ref[t] = jnp.concatenate(rows + [packed], axis=0).astype(BF16)


def last_kernel(scale, got_ref, backup_ref, grad_ref):
    totals = [jnp.zeros((8, 128), F32)] * 2
    for pair in range(32):
        blocks = [got_ref[2 * pair].astype(F32), got_ref[2 * pair + 1].astype(F32)]
        for c in range(2):
            totals[c] = totals[c] + blocks[c][24:]
        for k in range(2):
            flat = jnp.concatenate([block[12 * k : 12 * k + 12] for block in blocks], axis=0)
            for i in range(3):
                tile = 3 * pair + i
                backup_ref[tile // 32, k, pl.ds(tile % 32 * 8, 8), :] = flat[8 * i : 8 * i + 8]
    group = lane_group((8, 128))
    for g in range(3):
        low = pltpu.roll(totals[0], (-32 * g) % 128, 1)
        high = pltpu.roll(totals[1], (32 - 32 * g) % 128, 1)
        grad_ref[pl.ds(8 * g, 8), :] = (jnp.where(group == 0, low, high) * scale)[:, :64]


def term_kernel(core_ref, pre_ref, g0, g1, g2, g3, own_ref, other_ref, right_ref):
    @pl.when(pl.program_id(0) == 0)
    def _():
        act = gelu_value(pre_ref[...].astype(F32)).T
        low = jnp.concatenate([act, jnp.zeros((128, 192), F32)], axis=1)
        lane = lax.broadcasted_iota(jnp.int32, (128, 256), 1)
        mine = core_ref[0]
        for q in range(4):
            a = pltpu.roll(low, 32 * q, 1)
            b = pltpu.roll(low, (32 * q - 32) % 256, 1)
            keep, send = jnp.where(mine == 0, a, b), jnp.where(mine == 0, b, a)
            send = pltpu.roll(send, 128, 1)
            both = jnp.where(
                lane // 32 == q, keep, jnp.where(lane // 32 == q + 4, send, 0.0)
            )
            right_ref[q] = both.astype(BF16)

    total = None
    for q, g in enumerate((g0, g1, g2, g3)):
        part = lax.dot_general(
            g[...], right_ref[q], (((0,), (0,)), ((), ())), preferred_element_type=F32
        )
        total = part if total is None else total + part
    for p in range(2):
        for yh in range(2):
            for x in range(4):
                at = ((p * 2 + yh) * 4 + x) * 24
                own_ref[x, yh, p] = total[at : at + 24, :128]
                other_ref[x, yh, p] = total[at : at + 24, 128:]


def back_kernel(place_ref, own_ref, other_ref, pre_ref, g0, g1, g2, g3, out_ref, weight_ref, acc_ref):
    step = pl.program_id(0)

    @pl.when(step == 0)
    def _():
        acc_ref[...] = jnp.zeros_like(acc_ref)

    for p in range(2):
        for yh in range(2):
            j = yh ^ place_ref[1]
            for x in range(4):
                at = ((p * 2 + yh) * 4 + x) * 24
                weight_ref[pl.ds(at, 24), :128] = own_ref[x, j, p].astype(F32)
                weight_ref[pl.ds(at, 24), 128:] = other_ref[x, j, p].astype(F32)
    weight = weight_ref[...].astype(BF16)
    for q, g in enumerate((g0, g1, g2, g3)):
        acc_ref[q] += jnp.dot(g[...], weight, preferred_element_type=F32)

    @pl.when(step == pl.num_programs(0) - 1)
    def _():
        lane = lax.broadcasted_iota(jnp.int32, (128, 256), 1)
        total = jnp.zeros((128, 256), F32)
        for q in range(4):
            total = jnp.where(lane // 32 % 4 == q, acc_ref[q], total)
        halves = []
        for c in range(2):
            half = total[:, 128 * c : 128 * c + 128]
            half = half + pltpu.roll(half, 64, 1)
            halves.append(half + pltpu.roll(half, 32, 1))
        is_low = lax.broadcasted_iota(jnp.int32, (128, 128), 1) // 32 % 2 == place_ref[0]
        both = jnp.where(is_low, halves[0], halves[1]).T[:64]
        out_ref[...] = (both * gelu_slope(pre_ref[...].astype(F32))).astype(BF16)


def call(kernel, out_shape, in_specs, **kwargs):
    return pl.pallas_call(
        kernel,
        out_shape=out_shape,
        in_specs=in_specs,
        out_specs=jax.tree.map(lambda _: VMEM, out_shape),
        compiler_params=pltpu.CompilerParams(vmem_limit_bytes=LIMIT),
        **kwargs,
    )


def grad_specs():
    return [pl.BlockSpec((128, 384), lambda s, c, q=q: (0, q * 8 + s)) for q in range(4)]


def shards(grad_out, pre_act, down_rows, states, partner_hosts, slice_start):
    axes = ("hst", "dev")
    core = lax.axis_index("hst") % 2
    x = lax.axis_index("dev") % 4
    yh = lax.axis_index("dev") // 4

    def flip(array, bits):
        return lax.ppermute(array, axes, [(i, i ^ bits) for i in range(512)])

    shape = jax.ShapeDtypeStruct
    send1 = call(first_kernel, shape((64, 24, 128), BF16), [SMEM, VMEM, VMEM])(
        slice_start, states, down_rows
    )
    got1 = lax.all_to_all(send1, "hst", 0, 0, tiled=True)

    blocks = pl.BlockSpec((4, 2, 2, 24, 128), lambda s, c: (0, 0, s, 0, 0))
    fixed = pl.BlockSpec((64, 128), lambda s, c: (0, 0))
    keep, send = pl.pallas_call(
        term_kernel,
        out_shape=[shape((4, 2, 16, 24, 128), F32)] * 2,
        grid_spec=pltpu.PrefetchScalarGridSpec(
            num_scalar_prefetch=1,
            grid=(8,),
            in_specs=[fixed] + grad_specs(),
            out_specs=[blocks, blocks],
            scratch_shapes=[pltpu.VMEM((4, 128, 256), BF16)],
        ),
        compiler_params=pltpu.CompilerParams(vmem_limit_bytes=LIMIT),
    )(core[None], pre_act.T, *[grad_out] * 4)
    arrived = flip(send, 8)

    def pick(k):
        return keep[x ^ k] + arrived[x ^ k]

    leaving = [pick(k).astype(jnp.float16) for k in (1, 3, 2)]
    parts = [flip(part, k) for part, k in zip(leaving, (1, 3, 2))]
    got1, _ = lax.optimization_barrier((got1, leaving))
    summed = pick(0)
    for part in parts:
        summed = summed + part.astype(F32)
    mine = summed[yh]
    other = flip((summed[1 - yh] * 0.25).astype(jnp.float16), 4)

    sources = jnp.arange(64, dtype=jnp.int32)
    matches = partner_hosts[:, :, None] == sources[None, None, :]
    inverse = jnp.sum(jnp.where(matches, sources[:, None, None], 0), axis=0)
    held = call(weight_kernel, shape((16, 24, 128), BF16), [VMEM])(got1)
    held, _ = lax.optimization_barrier((held, parts[0]))
    across = flip(held, 4)
    inverse, _ = lax.optimization_barrier((inverse, across))
    send2 = call(second_kernel, shape((64, 32, 128), BF16), [SMEM, VMEM, VMEM, VMEM])(
        inverse, got1, mine, other.astype(F32)
    )
    got2 = lax.all_to_all(send2, "hst", 0, 0, tiled=True)
    backup, grad_bucket = call(
        functools.partial(last_kernel, 1.0 / 512),
        [shape((3, 2, CKR, 128), F32), shape((24, 64), F32)],
        [VMEM],
    )(got2)

    held, across, _ = lax.optimization_barrier((held, across, send2))
    pair = jnp.concatenate([held, across]).reshape(768, 128)
    lines = [[0, 1, 2, 3], [4, 5, 6, 7]]
    own = lax.all_gather(pair, "dev", axis=0, tiled=True, axis_index_groups=lines)
    own = own.reshape(4, 2, 16, 24, 128)
    far = flip(own, 8)
    wide = pl.BlockSpec((4, 2, 2, 24, 128), lambda s, c: (0, 0, s, 0, 0))
    grad_pre = pl.pallas_call(
        back_kernel,
        out_shape=shape((64, 128), BF16),
        grid_spec=pltpu.PrefetchScalarGridSpec(
            num_scalar_prefetch=1,
            grid=(8,),
            in_specs=[wide, wide, fixed] + grad_specs(),
            out_specs=fixed,
            scratch_shapes=[pltpu.VMEM((384, 256), F32), pltpu.VMEM((4, 128, 256), F32)],
        ),
        compiler_params=pltpu.CompilerParams(vmem_limit_bytes=LIMIT),
    )(jnp.stack([core, yh]), own, far, pre_act.T, *[grad_out] * 4)
    return (grad_bucket, grad_pre.T, backup)


def solution(mesh):
    return jax.shard_map(
        shards,
        mesh=mesh,
        in_specs=(
            P(("hst", "dev"), None),
            P(("hst", "dev"), None),
            P(("hst", "dev"), None),
            P(None, ("hst", "dev"), None),
            P(),
            P("hst", "dev"),
        ),
        out_specs=(
            P(("hst", "dev"), None),
            P(("hst", "dev"), None),
            P(None, None, ("hst", "dev"), None),
        ),
        check_vma=False,
    )
```
